32 devices in a mesh: groups: 2 (over y), dp: 4 (over x, core), tensor: 4 (over z).
Axes of the slice: x: 2, y: 2, z: 4, core: 2. Of those that a mesh axis runs over, the one named last changes fastest.
Arguments:
- hidden_in: bfloat16 [256, 8192], P(('groups', 'tensor'), 'dp'), parts along dimension 0, may hold values from -45 to 45
- gain: float32 [8192], P('dp'), may hold values from 0.25 to 1.75
- w_gate: bfloat16 [8192, 14336], P('dp', 'tensor'), may hold values from -0.0625 to 0.0625
- w_up: bfloat16 [8192, 14336], P('dp', 'tensor'), may hold values from -0.0625 to 0.0625
- w_down: bfloat16 [14336, 8192], P('tensor', 'dp'), may hold values from -0.046875 to 0.046875
- exit_layer: int32 [256], P(('groups', 'tensor')), parts along dimension 0, may hold values from 1 to 80, as said below
Outputs:
- mixed: bfloat16 [256, 8192], P(('groups', 'tensor'), 'dp'), parts along dimension 0
The draws below stay inside these ranges and needn't reach their ends.
There are 2 independent parts, one for each index of `groups`. The reference program is written for one: setup_inputs(seed, part) draws one part's arguments, and reference() takes and returns one part's arrays. A program takes and returns all parts, laid end to end along the dimension named above; an argument that names none is the same for every part. Nothing has to cross between parts.
Inputs may be any that keep to these rules, and one draw needn't show every extreme that they name: In each aligned block of 32 rows (the rows of one index of tensor) at most 16 rows have exit_layer above 40; some block has exactly 16, and all blocks of a part may have exactly 16.
All inputs are finite; a program needn't handle non-finite values.
Results may differ from the reference program's by a relative error of at most 0.0055.
Values may be sent and summed in bfloat16 or wider, within the bound.
A program may use at most 128 MiB of HBM per device.

```python
import jax
import jax.numpy as jnp
from jax import lax

D = 8192
NUM_LAYERS = 80
FW = 14336
LAYER = 40
ROW_T = 32
SURV_MAX = 16
ROWS = 128
N_DP = 4
N_TENSOR = 4


def draw_hidden_in(key, part):
    key = jax.random.fold_in(key, 11)
    first, second, third = jax.random.split(key, 3)
    columns = jnp.arange(D, dtype=jnp.float32)
    col_scale = jnp.exp(jnp.log(3.0) * columns / (D - 1)) * jax.random.uniform(second, (D,), jnp.float32, 0.7, 1.4)
    base = jax.random.truncated_normal(first, -3.5, 3.5, (ROWS, D), jnp.float32)
    row_scale = jnp.exp(jax.random.uniform(third, (ROWS, 1), jnp.float32, jnp.log(0.5), jnp.log(3.0)))
    return (base * row_scale * col_scale).astype(jnp.bfloat16)


def draw_exit_layer(key, part):
    key = jax.random.fold_in(key, 23)
    k_count, k_pick, k_perm, k_late, k_early = jax.random.split(key, 5)
    blocks = ROWS // ROW_T
    counts = jax.random.randint(k_count, (blocks,), 1, SURV_MAX + 1)
    busiest = jax.random.randint(k_pick, (), 0, blocks)
    counts = jnp.where(jnp.arange(blocks) == busiest, SURV_MAX, counts)
    counts = jnp.where(part % 2 == 0, SURV_MAX, counts)
    perm_keys = jax.random.split(k_perm, blocks)
    orders = jax.vmap(lambda k: jax.random.permutation(k, ROW_T))(perm_keys)
    survive = (orders < counts[:, None]).reshape(ROWS)
    late = jax.random.randint(k_late, (ROWS,), LAYER + 1, NUM_LAYERS + 1)
    early = jax.random.randint(k_early, (ROWS,), 1, LAYER + 1)
    return jnp.where(survive, late, early).astype(jnp.int32)


def steps_of(stream_key, shape, shards, low, top_value):
    factor_of, own = 1.0, jax.random.fold_in(stream_key, 6)
    for position, parts in shards:
        heights = jnp.exp(jax.random.uniform(jax.random.fold_in(own, position), (parts,), jnp.float32, low / len(shards), top_value / len(shards)))
        factor_of = factor_of * jnp.repeat(heights, shape[position] // parts).reshape([-1 if axis == position else 1 for axis in range(len(shape))])
    return factor_of


def bell_draw(rng, dims, deviation, bound, cuts=(), kind=jnp.bfloat16):
    result = deviation * jax.random.normal(rng, dims, jnp.float32)
    if cuts:
        result = result * steps_of(rng, dims, cuts, -0.22, 0.18)
    return jnp.clip(result, -bound, bound).astype(kind)


def setup_inputs(seed: int = 0, part: int = 0) -> dict:
    key_list = jax.random.split(jax.random.key(seed), 7)
    part_splits = jax.random.split(jax.random.fold_in(key_list[6], part), 7)
    hidden_in = draw_hidden_in(jax.random.fold_in(jax.random.fold_in(key_list[6], part), 71), part)
    gain = jnp.clip(1.0 + 0.15 * jax.random.normal(key_list[1], (D,), jnp.float32), 0.25, 1.75)
    w_gate = bell_draw(key_list[2], (D, FW), D ** -0.5, 0.0625, ((0, 4), (1, 4)))
    w_up = bell_draw(key_list[3], (D, FW), D ** -0.5, 0.0625, ((0, 4), (1, 4)))
    w_down = bell_draw(key_list[4], (FW, D), FW ** -0.5, 0.046875, ((0, 4), (1, 4)))
    exit_layer = draw_exit_layer(jax.random.fold_in(jax.random.fold_in(key_list[6], part), 71), part)
    return {"hidden_in": hidden_in, "gain": gain, "w_gate": w_gate, "w_up": w_up, "w_down": w_down, "exit_layer": exit_layer}


EPS = 1e-05

def reference(hidden_in, gain, w_gate, w_up, w_down, exit_layer):
    values = hidden_in.astype(jnp.float32)
    inv_rms = lax.rsqrt(lax.optimization_barrier(jnp.sum(values * values, axis=1)) / D + EPS)
    scaled = (values * gain).astype(jnp.bfloat16)
    feature_group = D // N_DP

    def add_features(totals, index):
        start = (index * feature_group).astype(jnp.int32)
        piece = lax.dynamic_slice_in_dim(scaled, start, feature_group, 1)
        gate_rows = lax.dynamic_slice_in_dim(w_gate, start, feature_group, 0)
        up_rows = lax.dynamic_slice_in_dim(w_up, start, feature_group, 0)
        gate_term = jnp.dot(piece, gate_rows, preferred_element_type=jnp.float32).astype(jnp.bfloat16)
        up_term = jnp.dot(piece, up_rows, preferred_element_type=jnp.float32).astype(jnp.bfloat16)
        gate_term, up_term = lax.optimization_barrier((gate_term, up_term))
        return ((totals[0] + gate_term.astype(jnp.float32), totals[1] + up_term.astype(jnp.float32)), None)
    zeros_wide = jnp.zeros((ROWS, FW), jnp.float32)
    (gate_raw, up_raw), _ = lax.scan(add_features, (zeros_wide, zeros_wide), jnp.arange(N_DP, dtype=jnp.int32))
    act = (jax.nn.silu(gate_raw * inv_rms[:, None]) * (up_raw * inv_rms[:, None])).astype(jnp.bfloat16)
    group_size = FW // N_TENSOR

    def add_group(total, index):
        start = (index * group_size).astype(jnp.int32)
        part = lax.dynamic_slice_in_dim(act, start, group_size, 1)
        block = lax.dynamic_slice_in_dim(w_down, start, group_size, 0)
        term = jnp.dot(part, block, preferred_element_type=jnp.float32).astype(jnp.bfloat16)
        term = lax.optimization_barrier(term)
        return (total + term.astype(jnp.float32), None)
    ffn_out, _ = lax.scan(add_group, jnp.zeros((ROWS, D), jnp.float32), jnp.arange(N_TENSOR, dtype=jnp.int32))
    kept_mask = exit_layer > LAYER
    return (values + jnp.where(kept_mask[:, None], ffn_out, jnp.float32(0.0))).astype(jnp.bfloat16)
```

```python
import functools

import jax
import jax.numpy as jnp
from jax import lax
from jax.experimental import pallas as pl
from jax.experimental.pallas import tpu as pltpu
from jax.sharding import PartitionSpec as P

D = 8192
LAYER = 40
SURV_MAX = 16
EPS = 1e-05
MESH = pl.DeviceIdType.MESH
F32 = jnp.float32
BF16 = jnp.bfloat16


def kernel(
    n_dp, n_t, nj, hid, gain, exits, w_gate, w_up, w_down, out,
    hid_v, gain_v, exit_v, wg_v, wu_v, wd_v,
    rows_v, xs, sq, sq_in, inv_v, sel_v,
    part, core_in, chip_sum, chip_in, act_v, acc, z_out, z_in,
    in_sem, wg_sem, wu_sem, wd_sem, ag_s, ag_r, sq_s, sq_r,
    a_s, a_r, b_s, b_r, c_s, c_r, p_s, p_r, f_s, f_r, z_s, z_r,
):
    n_x = n_dp // 2
    me_dp = lax.axis_index("dp")
    me_t = lax.axis_index("tensor")
    x = me_dp // 2
    c = me_dp % 2
    other = x * 2 + (1 - c)
    slots, d_l = SURV_MAX, hid.shape[1]
    tok = hid.shape[0]
    n_rows = n_t * slots
    half = n_rows // 2
    blk = n_rows // n_dp
    width = wg_v.shape[2]

    def remote(src, dst, send, recv, **where):
        return pltpu.make_async_remote_copy(
            src_ref=src, dst_ref=dst, send_sem=send, recv_sem=recv,
            device_id=where, device_id_type=MESH,
        )

    barrier = pltpu.get_barrier_semaphore()
    for o in range(1, n_t):
        pl.semaphore_signal(barrier, inc=1, device_id={"tensor": (me_t + o) % n_t}, device_id_type=MESH)
    for o in range(1, n_dp):
        pl.semaphore_signal(barrier, inc=1, device_id={"dp": (me_dp + o) % n_dp}, device_id_type=MESH)

    small = [
        pltpu.make_async_copy(hid, hid_v, in_sem.at[0]),
        pltpu.make_async_copy(exits, exit_v, in_sem.at[1]),
        pltpu.make_async_copy(gain, gain_v, in_sem.at[2]),
    ]
    for cp in small:
        cp.start()

    def col(j):
        return pl.ds(pl.multiple_of(j * width, width), width) if nj > 1 else pl.ds(0, width)

    def gate_copy(j):
        return pltpu.make_async_copy(w_gate.at[:, col(j)], wg_v.at[j], wg_sem.at[j])

    def up_copy(j):
        return pltpu.make_async_copy(w_up.at[:, col(j)], wu_v.at[j], wu_sem.at[j])

    def down_copy(j):
        return pltpu.make_async_copy(w_down.at[col(j), :], wd_v.at[j], wd_sem.at[j])

    @pl.loop(0, nj)
    def _(j):
        gate_copy(j).start()
        up_copy(j).start()

    for cp in small:
        cp.wait()

    kept = exit_v[...] > LAYER
    r_id = lax.broadcasted_iota(jnp.int32, (tok, tok), 0)
    c_id = lax.broadcasted_iota(jnp.int32, (tok, tok), 1)
    tri = (r_id <= c_id).astype(F32)
    rank = jnp.dot(kept.astype(F32), tri, preferred_element_type=F32) - 1.0
    s_id = lax.broadcasted_iota(jnp.int32, (slots, tok), 0).astype(F32)
    kept_b = jnp.broadcast_to(kept.astype(F32), (slots, tok))
    sel = jnp.where(jnp.broadcast_to(rank, (slots, tok)) == s_id, kept_b, 0.0)
    sel_v[...] = sel
    rows_v[me_t] = jnp.dot(sel.astype(BF16), hid_v[...], preferred_element_type=F32).astype(BF16)

    pl.semaphore_wait(barrier, n_t + n_dp - 2)

    def ag_copy(o, src):
        return remote(rows_v.at[src], rows_v.at[src], ag_s.at[o - 1], ag_r.at[o - 1], tensor=(me_t + o) % n_t)

    for o in range(1, n_t):
        ag_copy(o, me_t).start()

    def take_rows(t):
        v = rows_v[t].astype(F32)
        xs[t] = (v * gain_v[...]).astype(BF16)
        total = v[:, :128] * v[:, :128]
        for k in range(1, d_l // 128):
            piece = v[:, k * 128:(k + 1) * 128]
            total = total + piece * piece
        sq[pl.ds(pl.multiple_of(t * slots, slots), slots), :] = total

    take_rows(me_t)
    for o in range(1, n_t):
        src = (me_t + n_t - o) % n_t
        ag_copy(o, src).wait_recv()
        take_rows(src)

    def place(d):
        return (d % 2) * n_x + d // 2

    def rows_of(b):
        return pl.ds(pl.multiple_of(b * blk, blk), blk)

    def sq_copy(o):
        d = (me_dp + o) % n_dp
        return remote(sq.at[rows_of(place(d)), :], sq_in.at[o - 1], sq_s.at[o - 1], sq_r.at[o - 1], dp=d)

    for o in range(1, n_dp):
        sq_copy(o).start()

    acc[...] = jnp.zeros_like(acc)

    mine = c * n_x + x
    lead = max(nj, 4)

    def a_copy(j):
        return remote(part.at[j, 1 - c], core_in.at[j], a_s.at[j], a_r.at[j], dp=other)

    def b_copy(j, o):
        xd = (x + o) % n_x
        return remote(chip_sum.at[j, xd], chip_in.at[j, o - 1], b_s.at[j, o - 1], b_r.at[j, o - 1], dp=xd * 2 + c)

    def c_copy(j, o, b):
        xd = (x + o) % n_x
        return remote(act_v.at[j, b], act_v.at[j, b], c_s.at[j, o - 1], c_r.at[j, o - 1], dp=xd * 2 + c)

    def p_copy(j, b):
        return remote(act_v.at[j, b], act_v.at[j, b], p_s.at[j], p_r.at[j], dp=other)

    def f_copy(j, o, b):
        return remote(act_v.at[j, b], act_v.at[j, b], f_s.at[j, o - 1], f_r.at[j, o - 1], dp=other)

    @pl.loop(0, nj + lead)
    def _(it):
        @pl.when(it < nj)
        def _():
            j = it
            down_copy(j).start()
            xv = xs[...].reshape(n_rows, d_l)
            for m, (copy, w) in enumerate(((gate_copy, wg_v), (up_copy, wu_v))):
                copy(j).wait()
                p = jnp.dot(xv, w[j], preferred_element_type=F32).astype(BF16)
                part[j, 0, m] = p[:half]
                part[j, 1, m] = p[half:]
            a_copy(j).start()

        @pl.when((it >= 1) & (it < nj + 1))
        def _():
            j = it - 1
            a_copy(j).wait_recv()
            s = part[j, c].astype(F32) + core_in[j].astype(F32)
            for b in range(n_x):
                chip_sum[j, b] = s[:, b * blk:(b + 1) * blk].astype(BF16)
            for o in range(1, n_x):
                b_copy(j, o).start()

        @pl.when(it == 2)
        def _():
            total = sq[rows_of(mine), :]
            for o in range(1, n_dp):
                sq_copy(o).wait_recv()
                total = total + sq_in[o - 1]
            ms = jnp.sum(total, axis=1, keepdims=True) / D
            inv_v[...] = jnp.broadcast_to(lax.rsqrt(ms + EPS), inv_v.shape)

        @pl.when((it >= 2) & (it < nj + 2))
        def _():
            j = it - 2
            t = part[j, c, :, rows_of(x), :].astype(F32) + core_in[j, :, rows_of(x), :].astype(F32)
            for o in range(1, n_x):
                b_copy(j, o).wait_recv()
                t = t + chip_in[j, o - 1].astype(F32)
            inv = inv_v[:, :1]
            g = t[0] * inv
            u = t[1] * inv
            act_v[j, mine] = (g / (1.0 + jnp.exp(-g)) * u).astype(BF16)
            for o in range(1, n_x):
                c_copy(j, o, mine).start()
            p_copy(j, mine).start()

        @pl.when((it >= 3) & (it < nj + 3))
        def _():
            j = it - 3
            for o in range(1, n_x):
                b = c * n_x + (x + n_x - o) % n_x
                c_copy(j, o, b).wait_recv()
                f_copy(j, o, b).start()

        @pl.when(it >= lead)
        def _():
            j = it - lead
            p_copy(j, (1 - c) * n_x + x).wait_recv()
            for o in range(1, n_x):
                f_copy(j, o, (1 - c) * n_x + (x + n_x - o) % n_x).wait_recv()
            down_copy(j).wait()
            a = act_v[j].reshape(n_rows, width)
            acc[...] += jnp.dot(a, wd_v[j], preferred_element_type=F32)

    def z_copy(o):
        t = (me_t + o) % n_t
        return remote(z_out.at[t], z_in.at[o - 1], z_s.at[o - 1], z_r.at[o - 1], tensor=t)

    for o in range(1, n_t):
        t = (me_t + o) % n_t
        z_out[t] = acc[pl.ds(pl.multiple_of(t * slots, slots), slots), :].astype(BF16)
        z_copy(o).start()
    total = acc[pl.ds(pl.multiple_of(me_t * slots, slots), slots), :].astype(BF16).astype(F32)

    @pl.loop(0, nj)
    def _(j):
        a_copy(j).wait_send()
        p_copy(j, mine).wait_send()
        for o in range(1, n_x):
            b_copy(j, o).wait_send()
            c_copy(j, o, mine).wait_send()
            f_copy(j, o, c * n_x + (x + n_x - o) % n_x).wait_send()

    for o in range(1, n_t):
        ag_copy(o, me_t).wait_send()
    for o in range(1, n_dp):
        sq_copy(o).wait_send()

    for o in range(1, n_t):
        z_copy(o).wait_recv()
        total = total + z_in[o - 1].astype(F32)
    for o in range(1, n_t):
        z_copy(o).wait_send()

    sel_b = sel_v[...].astype(BF16)
    back = (((0,), (0,)), ((), ()))
    high = total.astype(BF16)
    low = (total - high.astype(F32)).astype(BF16)
    branch = lax.dot_general(sel_b, high, back, preferred_element_type=F32)
    branch = branch + lax.dot_general(sel_b, low, back, preferred_element_type=F32)
    out[...] = (hid_v[...].astype(F32) + branch).astype(BF16)


def solution(mesh):
    n_dp, n_t = mesh.shape["dp"], mesh.shape["tensor"]
    n_x = n_dp // 2

    def local(hidden_in, gain, w_gate, w_up, w_down, exit_layer):
        tok, d_l = hidden_in.shape
        f_l = w_gate.shape[1]
        width = 512 if f_l % 512 == 0 else f_l
        nj = f_l // width
        n_rows = n_t * SURV_MAX
        half, blk = n_rows // 2, n_rows // n_dp
        nx1 = max(n_x - 1, 1)
        any_spec = pl.BlockSpec(memory_space=pl.ANY)
        dma = pltpu.SemaphoreType.DMA
        vmem = pltpu.VMEM
        return pl.pallas_call(
            functools.partial(kernel, n_dp, n_t, nj),
            out_shape=jax.ShapeDtypeStruct((tok, d_l), BF16),
            in_specs=[any_spec] * 6,
            out_specs=pl.BlockSpec(memory_space=pltpu.VMEM),
            scratch_shapes=[
                vmem((tok, d_l), BF16),
                vmem((1, d_l), F32),
                vmem((1, tok), jnp.int32),
                vmem((nj, d_l, width), BF16),
                vmem((nj, d_l, width), BF16),
                vmem((nj, width, d_l), BF16),
                vmem((n_t, SURV_MAX, d_l), BF16),
                vmem((n_t, SURV_MAX, d_l), BF16),
                vmem((n_rows, 128), F32),
                vmem((n_dp - 1, blk, 128), F32),
                vmem((blk, 128), F32),
                vmem((SURV_MAX, tok), F32),
                vmem((nj, 2, 2, half, width), BF16),
                vmem((nj, 2, half, width), BF16),
                vmem((nj, n_x, 2, blk, width), BF16),
                vmem((nj, nx1, 2, blk, width), BF16),
                vmem((nj, n_dp, blk, width), BF16),
                vmem((n_rows, d_l), F32),
                vmem((n_t, SURV_MAX, d_l), BF16),
                vmem((n_t - 1, SURV_MAX, d_l), BF16),
                dma((3,)), dma((nj,)), dma((nj,)), dma((nj,)),
                dma((n_t - 1,)), dma((n_t - 1,)), dma((n_dp - 1,)), dma((n_dp - 1,)),
                dma((nj,)), dma((nj,)), dma((nj, nx1)), dma((nj, nx1)),
                dma((nj, nx1)), dma((nj, nx1)), dma((nj,)), dma((nj,)),
                dma((nj, nx1)), dma((nj, nx1)), dma((n_t - 1,)), dma((n_t - 1,)),
            ],
            compiler_params=pltpu.CompilerParams(
                collective_id=0, has_side_effects=True, vmem_limit_bytes=60 * 1024 * 1024
            ),
            name="ffn_block",
        )(hidden_in, gain.reshape(1, -1), exit_layer.reshape(1, -1), w_gate, w_up, w_down)

    placed = (
        P(("groups", "tensor"), "dp"),
        P("dp"),
        P("dp", "tensor"),
        P("dp", "tensor"),
        P("tensor", "dp"),
        P(("groups", "tensor")),
    )
    return jax.shard_map(
        local, mesh=mesh, in_specs=placed, out_specs=P(("groups", "tensor"), "dp"), check_vma=False
    )
```

```python
import functools

import jax
import jax.numpy as jnp
from jax import lax
from jax.experimental import pallas as pl
from jax.experimental.pallas import tpu as pltpu
from jax.sharding import PartitionSpec as P

D = 8192
LAYER = 40
SURV_MAX = 16
EPS = 1e-05
LAG = 2
MESH = pl.DeviceIdType.MESH
F32 = jnp.float32
BF16 = jnp.bfloat16


def kernel(
    n_dp, n_t, nj, hid, gain, exits, w_gate, w_up, w_down, out,
    hid_v, gain_v, exit_v, wg_v, wu_v, wd_v,
    rows_v, xs, sq, sq_in, inv_v, sel_v,
    part, core_in, chip_sum, chip_in, act_v, acc, z_out, z_in,
    in_sem, wg_sem, wu_sem, wd_sem, ag_s, ag_r, sq_s, sq_r,
    a_s, a_r, b_s, b_r, c_s, c_r, p_s, p_r, f_s, f_r, z_s, z_r,
):
    n_x = n_dp // 2
    me_dp = lax.axis_index("dp")
    me_t = lax.axis_index("tensor")
    x = me_dp // 2
    c = me_dp % 2
    other = x * 2 + (1 - c)
    slots, d_l = SURV_MAX, hid.shape[1]
    tok = hid.shape[0]
    n_rows = n_t * slots
    half = n_rows // 2
    blk = n_rows // n_dp
    width = wg_v.shape[2]

    def remote(src, dst, send, recv, **where):
        return pltpu.make_async_remote_copy(
            src_ref=src, dst_ref=dst, send_sem=send, recv_sem=recv,
            device_id=where, device_id_type=MESH,
        )

    barrier = pltpu.get_barrier_semaphore()
    for o in range(1, n_t):
        pl.semaphore_signal(barrier, inc=1, device_id={"tensor": (me_t + o) % n_t}, device_id_type=MESH)
    for o in range(1, n_dp):
        pl.semaphore_signal(barrier, inc=1, device_id={"dp": (me_dp + o) % n_dp}, device_id_type=MESH)

    small = [
        pltpu.make_async_copy(hid, hid_v, in_sem.at[0]),
        pltpu.make_async_copy(exits, exit_v, in_sem.at[1]),
        pltpu.make_async_copy(gain, gain_v, in_sem.at[2]),
    ]
    for cp in small:
        cp.start()

    def col(j):
        return pl.ds(pl.multiple_of(j * width, width), width) if nj > 1 else pl.ds(0, width)

    def gate_copy(j):
        return pltpu.make_async_copy(w_gate.at[:, col(j)], wg_v.at[j], wg_sem.at[j])

    def up_copy(j):
        return pltpu.make_async_copy(w_up.at[:, col(j)], wu_v.at[j], wu_sem.at[j])

    def down_copy(j):
        return pltpu.make_async_copy(w_down.at[col(j), :], wd_v.at[j], wd_sem.at[j])

    @pl.loop(0, nj)
    def _(j):
        gate_copy(j).start()
        up_copy(j).start()

    for cp in small:
        cp.wait()

    kept = exit_v[...] > LAYER
    r_id = lax.broadcasted_iota(jnp.int32, (tok, tok), 0)
    c_id = lax.broadcasted_iota(jnp.int32, (tok, tok), 1)
    tri = (r_id <= c_id).astype(F32)
    rank = jnp.dot(kept.astype(F32), tri, preferred_element_type=F32) - 1.0
    s_id = lax.broadcasted_iota(jnp.int32, (slots, tok), 0).astype(F32)
    kept_b = jnp.broadcast_to(kept.astype(F32), (slots, tok))
    sel = jnp.where(jnp.broadcast_to(rank, (slots, tok)) == s_id, kept_b, 0.0)
    sel_v[...] = sel
    rows_v[me_t] = jnp.dot(sel.astype(BF16), hid_v[...], preferred_element_type=F32).astype(BF16)

    pl.semaphore_wait(barrier, n_t + n_dp - 2)

    def ag_copy(o, src):
        return remote(rows_v.at[src], rows_v.at[src], ag_s.at[o - 1], ag_r.at[o - 1], tensor=(me_t + o) % n_t)

    for o in range(1, n_t):
        ag_copy(o, me_t).start()

    def take_rows(t):
        v = rows_v[t].astype(F32)
        xs[t] = (v * gain_v[...]).astype(BF16)
        total = v[:, :128] * v[:, :128]
        for k in range(1, d_l // 128):
            piece = v[:, k * 128:(k + 1) * 128]
            total = total + piece * piece
        sq[pl.ds(pl.multiple_of(t * slots, slots), slots), :] = total

    take_rows(me_t)
    for o in range(1, n_t):
        src = (me_t + n_t - o) % n_t
        ag_copy(o, src).wait_recv()
        take_rows(src)

    def place(d):
        return (d % 2) * n_x + d // 2

    def rows_of(b):
        return pl.ds(pl.multiple_of(b * blk, blk), blk)

    def sq_copy(o):
        d = (me_dp + o) % n_dp
        return remote(sq.at[rows_of(place(d)), :], sq_in.at[o - 1], sq_s.at[o - 1], sq_r.at[o - 1], dp=d)

    for o in range(1, n_dp):
        sq_copy(o).start()

    acc[...] = jnp.zeros_like(acc)

    mine = c * n_x + x
    lead = max(nj, 2 * LAG + 1)

    def a_copy(j):
        return remote(part.at[j, 1 - c], core_in.at[j], a_s.at[j], a_r.at[j], dp=other)

    def b_copy(j, o):
        xd = (x + o) % n_x
        return remote(chip_sum.at[j, xd], chip_in.at[j, o - 1], b_s.at[j, o - 1], b_r.at[j, o - 1], dp=xd * 2 + c)

    def c_copy(j, o, b):
        xd = (x + o) % n_x
        return remote(act_v.at[j, b], act_v.at[j, b], c_s.at[j, o - 1], c_r.at[j, o - 1], dp=xd * 2 + c)

    def p_copy(j, b):
        return remote(act_v.at[j, b], act_v.at[j, b], p_s.at[j], p_r.at[j], dp=other)

    def f_copy(j, o, b):
        xd = (x + o) % n_x
        return remote(act_v.at[j, b], act_v.at[j, b], f_s.at[j, o - 1], f_r.at[j, o - 1], dp=xd * 2 + 1 - c)

    @pl.loop(0, nj + lead)
    def _(it):
        @pl.when(it < nj)
        def _():
            j = it
            down_copy(j).start()
            xv = xs[...].reshape(n_rows, d_l)
            for m, (copy, w) in enumerate(((gate_copy, wg_v), (up_copy, wu_v))):
                copy(j).wait()
                p = jnp.dot(xv, w[j], preferred_element_type=F32).astype(BF16)
                part[j, 0, m] = p[:half]
                part[j, 1, m] = p[half:]
            a_copy(j).start()

        @pl.when(it >= lead)
        def _():
            j = it - lead
            p_copy(j, (1 - c) * n_x + x).wait_recv()
            for o in range(1, n_x):
                xs_o = (x + n_x - o) % n_x
                c_copy(j, o, c * n_x + xs_o).wait_recv()
                f_copy(j, o, (1 - c) * n_x + xs_o).wait_recv()
            down_copy(j).wait()
            a = act_v[j].reshape(n_rows, width)
            acc[...] += jnp.dot(a, wd_v[j], preferred_element_type=F32)

        @pl.when((it >= LAG) & (it < nj + LAG))
        def _():
            j = it - LAG
            a_copy(j).wait_recv()
            s = part[j, c].astype(F32) + core_in[j].astype(F32)
            for b in range(n_x):
                chip_sum[j, b] = s[:, b * blk:(b + 1) * blk].astype(BF16)
            for o in range(1, n_x):
                b_copy(j, o).start()

        @pl.when(it == 2 * LAG)
        def _():
            total = sq[rows_of(mine), :]
            for o in range(1, n_dp):
                sq_copy(o).wait_recv()
                total = total + sq_in[o - 1]
            ms = jnp.sum(total, axis=1, keepdims=True) / D
            inv_v[...] = jnp.broadcast_to(lax.rsqrt(ms + EPS), inv_v.shape)

        @pl.when((it >= 2 * LAG) & (it < nj + 2 * LAG))
        def _():
            j = it - 2 * LAG
            t = part[j, c, :, rows_of(x), :].astype(F32) + core_in[j, :, rows_of(x), :].astype(F32)
            for o in range(1, n_x):
                b_copy(j, o).wait_recv()
                t = t + chip_in[j, o - 1].astype(F32)
            inv = inv_v[:, :1]
            g = t[0] * inv
            u = t[1] * inv
            act_v[j, mine] = (g / (1.0 + jnp.exp(-g)) * u).astype(BF16)
            for o in range(1, n_x):
                c_copy(j, o, mine).start()
                f_copy(j, o, mine).start()
            p_copy(j, mine).start()

    def z_copy(o):
        t = (me_t + o) % n_t
        return remote(z_out.at[t], z_in.at[o - 1], z_s.at[o - 1], z_r.at[o - 1], tensor=t)

    for o in range(1, n_t):
        t = (me_t + o) % n_t
        z_out[t] = acc[pl.ds(pl.multiple_of(t * slots, slots), slots), :].astype(BF16)
        z_copy(o).start()
    total = acc[pl.ds(pl.multiple_of(me_t * slots, slots), slots), :].astype(BF16).astype(F32)

    @pl.loop(0, nj)
    def _(j):
        a_copy(j).wait_send()
        p_copy(j, mine).wait_send()
        for o in range(1, n_x):
            b_copy(j, o).wait_send()
            c_copy(j, o, mine).wait_send()
            f_copy(j, o, mine).wait_send()

    for o in range(1, n_t):
        ag_copy(o, me_t).wait_send()
    for o in range(1, n_dp):
        sq_copy(o).wait_send()

    for o in range(1, n_t):
        z_copy(o).wait_recv()
        total = total + z_in[o - 1].astype(F32)
    for o in range(1, n_t):
        z_copy(o).wait_send()

    sel_b = sel_v[...].astype(BF16)
    back = (((0,), (0,)), ((), ()))
    high = total.astype(BF16)
    low = (total - high.astype(F32)).astype(BF16)
    branch = lax.dot_general(sel_b, high, back, preferred_element_type=F32)
    branch = branch + lax.dot_general(sel_b, low, back, preferred_element_type=F32)
    out[...] = (hid_v[...].astype(F32) + branch).astype(BF16)


def solution(mesh):
    n_dp, n_t = mesh.shape["dp"], mesh.shape["tensor"]
    n_x = n_dp // 2

    def local(hidden_in, gain, w_gate, w_up, w_down, exit_layer):
        tok, d_l = hidden_in.shape
        f_l = w_gate.shape[1]
        width = 512 if f_l % 512 == 0 else f_l
        nj = f_l // width
        n_rows = n_t * SURV_MAX
        half, blk = n_rows // 2, n_rows // n_dp
        nx1 = max(n_x - 1, 1)
        any_spec = pl.BlockSpec(memory_space=pl.ANY)
        dma = pltpu.SemaphoreType.DMA
        vmem = pltpu.VMEM
        return pl.pallas_call(
            functools.partial(kernel, n_dp, n_t, nj),
            out_shape=jax.ShapeDtypeStruct((tok, d_l), BF16),
            in_specs=[any_spec] * 6,
            out_specs=pl.BlockSpec(memory_space=pltpu.VMEM),
            scratch_shapes=[
                vmem((tok, d_l), BF16),
                vmem((1, d_l), F32),
                vmem((1, tok), jnp.int32),
                vmem((nj, d_l, width), BF16),
                vmem((nj, d_l, width), BF16),
                vmem((nj, width, d_l), BF16),
                vmem((n_t, SURV_MAX, d_l), BF16),
                vmem((n_t, SURV_MAX, d_l), BF16),
                vmem((n_rows, 128), F32),
                vmem((n_dp - 1, blk, 128), F32),
                vmem((blk, 128), F32),
                vmem((SURV_MAX, tok), F32),
                vmem((nj, 2, 2, half, width), BF16),
                vmem((nj, 2, half, width), BF16),
                vmem((nj, n_x, 2, blk, width), BF16),
                vmem((nj, nx1, 2, blk, width), BF16),
                vmem((nj, n_dp, blk, width), BF16),
                vmem((n_rows, d_l), F32),
                vmem((n_t, SURV_MAX, d_l), BF16),
                vmem((n_t - 1, SURV_MAX, d_l), BF16),
                dma((3,)), dma((nj,)), dma((nj,)), dma((nj,)),
                dma((n_t - 1,)), dma((n_t - 1,)), dma((n_dp - 1,)), dma((n_dp - 1,)),
                dma((nj,)), dma((nj,)), dma((nj, nx1)), dma((nj, nx1)),
                dma((nj, nx1)), dma((nj, nx1)), dma((nj,)), dma((nj,)),
                dma((nj, nx1)), dma((nj, nx1)), dma((n_t - 1,)), dma((n_t - 1,)),
            ],
            compiler_params=pltpu.CompilerParams(
                collective_id=0, has_side_effects=True, vmem_limit_bytes=60 * 1024 * 1024
            ),
            name="ffn_block",
        )(hidden_in, gain.reshape(1, -1), exit_layer.reshape(1, -1), w_gate, w_up, w_down)

    placed = (
        P(("groups", "tensor"), "dp"),
        P("dp"),
        P("dp", "tensor"),
        P("dp", "tensor"),
        P("tensor", "dp"),
        P(("groups", "tensor")),
    )
    return jax.shard_map(
        local, mesh=mesh, in_specs=placed, out_specs=P(("groups", "tensor"), "dp"), check_vma=False
    )
```
